1024 devices in a mesh: row: 32 (over y, z_lo, core), col: 32 (over x, z_hi).
Axes of the slice: x: 8, y: 8, z: 8 (z_hi: 4, z_lo: 2; z = z_hi * 2 + z_lo), core: 2. Of those that a mesh axis runs over, the one named last changes fastest.
Arguments:
- three_index: bfloat16 [32, 32, 8, 4, 128, 128], P('row', 'col'), may hold values from -0.015625 to 0.015625
- pair_list: int32 [32, 32, 8], P('row', 'col'), may hold values from 0 to 7
- block_offsets: int32 [32, 32, 8], P('row', 'col'), may hold values from 0 to 896, as said below
- block_count: int32 [32, 32], P('row', 'col'), may hold values from 1 to 8, as said below
- coefficients: bfloat16 [32768, 256], P('row'), may hold values from -6 to 6
Outputs:
- exchange_k: bfloat16 [32768, 32768], P('row', 'col')
The draws below stay inside these ranges and needn't reach their ends.
Inputs may be any that keep to these rules, and one draw needn't show every extreme that they name: `block_offsets`: a multiple of 128; the slots of one tile hold distinct pairs of offset and block index. `block_count`: slots at or past the count are ignored; some tile has 8.
All inputs are finite; a program needn't handle non-finite values.
Results may differ from the reference program's by a relative error of at most 0.025.
Values may be sent and summed in bfloat16 or wider, within the bound.
No kernel may reach another device: no remote copies, remote signals or barrier semaphores. Data moves between devices by JAX's collectives and lax.ppermute only.
A program may use at most 32 MiB of HBM per device.

```python
import jax
import jax.numpy as jnp
from jax import lax

BS = 128
NBLK = 8
OCC = 256
AUX = 4
MAXB = 8
TILE = 1024
RTILE = 1024
N = 32768
N_ROW = 32
N_COL = 32


def shared_pairs(key):
    row_blocks = TILE * N_COL // N_ROW // BS
    keys = jax.random.split(key, N_ROW * N_COL)
    chosen = jax.vmap(lambda k: jax.random.permutation(k, row_blocks * NBLK)[:MAXB])(keys)
    return chosen.reshape(N_ROW, N_COL, MAXB).astype(jnp.int32)


def draw_pair_list(key, part):
    return (shared_pairs(key) % NBLK).astype(jnp.int32)


def draw_block_offsets(key, part):
    return (shared_pairs(key) // NBLK * BS).astype(jnp.int32)


def draw_block_count(key, part):
    key = jax.random.fold_in(key, 5)
    first_key, second_key, third_key = jax.random.split(key, 3)
    grid_shape = (N_ROW, N_COL)
    counts = jnp.minimum(jax.random.randint(first_key, grid_shape, 1, MAXB + 1), jax.random.randint(second_key, grid_shape, 1, MAXB + 1))
    busiest = jax.random.randint(third_key, (), 0, N_ROW * N_COL)
    flat_counts = jnp.where(jnp.arange(N_ROW * N_COL) == busiest, MAXB, counts.reshape(-1))
    return flat_counts.reshape(grid_shape).astype(jnp.int32)


def block_scale(key, extent, shards, low, largest):
    loudness = 1.0
    for axis_at, shards_of in shards:
        heights = jax.random.uniform(jax.random.fold_in(jax.random.fold_in(key, 6), axis_at), (shards_of,), jnp.float32, low / len(shards), largest / len(shards))
        loudness = loudness * jnp.repeat(jnp.exp(heights), extent[axis_at] // shards_of).reshape((-1,) + (1,) * (len(extent) - 1 - axis_at))
    return loudness


def scatter_about(own_key, extent, width, limit, cuts=(), kind=jnp.bfloat16):
    entries = jax.random.normal(own_key, extent, jnp.float32) * width
    if len(cuts) > 0:
        entries = block_scale(own_key, extent, cuts, -0.22, 0.18) * entries
    return jnp.clip(entries, min=-limit, max=limit).astype(kind)


def setup_inputs(seed: int = 0) -> dict:
    key_list = jax.random.split(jax.random.key(seed), 6)
    return {
        "three_index": scatter_about(key_list[0], (N_ROW, N_COL, MAXB, AUX, BS, BS), 0.003, 0.015625, ((0, 32), (1, 32))),
        "pair_list": draw_pair_list(jax.random.fold_in(key_list[5], 71), 0),
        "block_offsets": draw_block_offsets(jax.random.fold_in(key_list[5], 71), 0),
        "block_count": draw_block_count(jax.random.fold_in(key_list[5], 71), 0),
        "coefficients": scatter_about(key_list[4], (N, OCC), 1.0, 6.0, ((0, 32),)),
    }


def reference(three_index, pair_list, block_offsets, block_count, coefficients):
    def tile_term(row_index, col_index):
        blocks = three_index[row_index, col_index]
        coef_rows = lax.dynamic_slice_in_dim(coefficients, (col_index * TILE).astype(jnp.int32), TILE, 0)
        term = jnp.zeros((AUX, RTILE, OCC), jnp.float32)
        for slot in range(MAXB):
            start = (pair_list[row_index, col_index, slot] * BS).astype(jnp.int32)
            nu_rows = lax.dynamic_slice_in_dim(coef_rows, start, BS, 0).astype(jnp.float32)
            part = jnp.einsum("pij,jo->pio", blocks[slot].astype(jnp.float32), nu_rows)
            live = (slot < block_count[row_index, col_index]).astype(jnp.float32)
            offset = block_offsets[row_index, col_index, slot].astype(jnp.int32)
            current = lax.dynamic_slice_in_dim(term, offset, BS, 1)
            term = lax.dynamic_update_slice_in_dim(term, current + live * part, offset, 1)
        return term.astype(jnp.bfloat16)

    def row_factor(row_index):
        def add_tile(total, col_index):
            return total + tile_term(row_index, col_index).astype(jnp.float32), None

        total, unused = lax.scan(add_tile, jnp.zeros((AUX, RTILE, OCC), jnp.float32), jnp.arange(N_COL, dtype=jnp.int32))
        return total.astype(jnp.bfloat16)

    factor = lax.map(row_factor, jnp.arange(N_ROW, dtype=jnp.int32))
    flat = jnp.transpose(factor, (0, 2, 1, 3)).reshape(N, AUX * OCC).astype(jnp.float32)

    def k_rows(row_index):
        rows = lax.dynamic_slice_in_dim(flat, (row_index * RTILE).astype(jnp.int32), RTILE, 0)
        return jnp.dot(rows, flat.T, precision=lax.Precision.HIGHEST).astype(jnp.bfloat16)

    blocks_out = lax.map(k_rows, jnp.arange(N_ROW, dtype=jnp.int32))
    return blocks_out.reshape(N, N)
```

```python
import jax
import jax.numpy as jnp
from jax import lax
from jax.experimental import pallas as pl
from jax.experimental.pallas import tpu as pltpu
from jax.sharding import PartitionSpec as P


def tile_term_kernel(pair_ref, offset_ref, count_ref, blocks_ref, coef_ref, term_ref, total):
    slot_total, aux_count, width, _ = blocks_ref.shape
    orbitals = coef_ref.shape[1]
    total[...] = jnp.zeros_like(total)
    for slot in range(slot_total):

        @pl.when(slot < count_ref[0])
        def _():
            first = pl.multiple_of(pair_ref[slot] * width, width)
            offset = pl.multiple_of(offset_ref[slot], width)
            nu_rows = coef_ref[pl.ds(first, width), :]
            for p in range(aux_count):
                columns = slice(p * orbitals, (p + 1) * orbitals)
                total[pl.ds(offset, width), columns] += jnp.dot(
                    blocks_ref[slot, p], nu_rows, preferred_element_type=jnp.float32
                )

    term_ref[...] = total[...].astype(term_ref.dtype)


def tile_term(blocks, pairs, offsets, count, coef):
    rows, orbitals = coef.shape
    columns = blocks.shape[1] * orbitals
    smem = pl.BlockSpec(memory_space=pltpu.SMEM)
    vmem = pl.BlockSpec(memory_space=pltpu.VMEM)
    return pl.pallas_call(
        tile_term_kernel,
        out_shape=jax.ShapeDtypeStruct((rows, columns), jnp.bfloat16),
        in_specs=[smem, smem, smem, vmem, vmem],
        out_specs=vmem,
        scratch_shapes=[pltpu.VMEM((rows, columns), jnp.float32)],
        compiler_params=pltpu.CompilerParams(vmem_limit_bytes=32 * 1024 * 1024),
    )(pairs, offsets, count, blocks, coef)


def spread(piece, axis):
    size = lax.axis_size(axis)
    copies = jnp.broadcast_to(piece[None], (size,) + piece.shape)
    copies = copies.reshape((size * piece.shape[0],) + piece.shape[1:])
    return lax.all_to_all(copies, axis, 0, 0, tiled=True)


def swap(piece, size):
    pairs = [(r * size + c, c * size + r) for r in range(size) for c in range(size)]
    return lax.ppermute(piece, ("row", "col"), pairs)


def on_device(three_index, pair_list, block_offsets, block_count, coefficients):
    size = lax.axis_size("row")
    part = coefficients.shape[0] // size

    own_coef = lax.dynamic_slice_in_dim(coefficients, lax.axis_index("col") * part, part, 0)
    column_coef = spread(swap(own_coef, size), "row")

    term = tile_term(
        three_index[0, 0], pair_list[0, 0], block_offsets[0, 0], block_count[0], column_coef
    )

    terms = lax.all_to_all(term, "col", 0, 0, tiled=True)
    terms = terms.reshape((size, part, term.shape[1]))
    factor = jnp.sum(terms, axis=0, dtype=jnp.float32).astype(jnp.bfloat16)

    swapped = swap(factor, size)
    factor, swapped = lax.optimization_barrier((factor, swapped))
    col_factor = lax.all_gather(swapped, "row", axis=0, tiled=True)
    row_factor = spread(factor, "col")
    tile = lax.dot_general(
        row_factor, col_factor, (((1,), (1,)), ((), ())), preferred_element_type=jnp.float32
    )
    return tile.astype(jnp.bfloat16)


def solution(mesh):
    return jax.shard_map(
        on_device,
        mesh=mesh,
        in_specs=(
            P("row", "col", None, None, None, None),
            P("row", "col", None),
            P("row", "col", None),
            P("row", "col"),
            P("row", None),
        ),
        out_specs=P("row", "col"),
        check_vma=False,
    )
```

```python
import jax
import jax.numpy as jnp
from jax import lax
from jax.experimental import pallas as pl
from jax.experimental.pallas import tpu as pltpu
from jax.sharding import PartitionSpec as P

DOUBLING = (16, 8, 4, 2)
PIECES = 1 << len(DOUBLING)
VMEM_LIMIT = 40 * 1024 * 1024


def member_bits(place):
    return sum(bit for k, bit in enumerate(DOUBLING) if place >> k & 1)


def tile_term_kernel(
    pair_ref, offset_ref, count_ref, core_ref, blocks_ref, mine_ref, other_ref, term_ref, total
):
    _, _, slot_total, aux_count, width, _ = blocks_ref.shape
    half, orbitals = mine_ref.shape
    in_half = half // width
    total[...] = jnp.zeros_like(total)
    for slot in range(slot_total):

        @pl.when(slot < count_ref[0, 0])
        def _():
            block = pair_ref[0, 0, slot]
            first = pl.multiple_of(lax.rem(block, in_half) * width, width)
            offset = pl.multiple_of(offset_ref[0, 0, slot], width)
            nu_rows = jnp.where(
                lax.div(block, in_half) == core_ref[0],
                mine_ref[pl.ds(first, width), :],
                other_ref[pl.ds(first, width), :],
            )
            for p in range(aux_count):
                columns = slice(p * orbitals, (p + 1) * orbitals)
                total[pl.ds(offset, width), columns] += jnp.dot(
                    blocks_ref[0, 0, slot, p], nu_rows, preferred_element_type=jnp.float32
                )

    term_ref[...] = total[...].astype(term_ref.dtype)


def tile_term(blocks, pairs, offsets, count, core, mine, other):
    rows, columns = 2 * mine.shape[0], blocks.shape[3] * mine.shape[1]
    smem = pl.BlockSpec(memory_space=pltpu.SMEM)
    vmem = pl.BlockSpec(memory_space=pltpu.VMEM)
    return pl.pallas_call(
        tile_term_kernel,
        out_shape=jax.ShapeDtypeStruct((rows, columns), jnp.bfloat16),
        in_specs=[smem, smem, smem, smem, vmem, vmem, vmem],
        out_specs=vmem,
        scratch_shapes=[pltpu.VMEM((rows, columns), jnp.float32)],
        compiler_params=pltpu.CompilerParams(vmem_limit_bytes=VMEM_LIMIT),
    )(pairs, offsets, count, core, blocks, mine, other)


def exchange_kernel(row_ref, row_factor_ref, mine_ref, other_ref, out_ref, col_factor):
    piece = col_factor.shape[0] // (2 * PIECES)

    @pl.when(pl.program_id(0) == 0)
    def _():
        for place in range(PIECES):
            member = row_ref[0] ^ member_bits(place)
            for held_ref, at in ((mine_ref, member), (other_ref, member ^ 1)):
                rows = pl.ds(pl.multiple_of(at * piece, piece), piece)
                col_factor[rows, :] = held_ref[place * piece : (place + 1) * piece, :]

    out_ref[...] = lax.dot_general(
        row_factor_ref[...],
        col_factor[...],
        (((1,), (1,)), ((), ())),
        preferred_element_type=jnp.float32,
    ).astype(out_ref.dtype)


def exchange_tile(row, row_factor, mine, other):
    rows, depth = row_factor.shape
    columns = 2 * mine.shape[0]
    step = rows // 4
    vmem = pl.BlockSpec(memory_space=pltpu.VMEM)
    return pl.pallas_call(
        exchange_kernel,
        grid=(rows // step,),
        out_shape=jax.ShapeDtypeStruct((rows, columns), jnp.bfloat16),
        in_specs=[
            pl.BlockSpec(memory_space=pltpu.SMEM),
            pl.BlockSpec((step, depth), lambda i: (i, 0)),
            vmem,
            vmem,
        ],
        out_specs=pl.BlockSpec((step, columns), lambda i: (i, 0)),
        scratch_shapes=[pltpu.VMEM((columns, depth), jnp.bfloat16)],
        compiler_params=pltpu.CompilerParams(vmem_limit_bytes=VMEM_LIMIT),
    )(row, row_factor, mine, other)


def copies_of(piece, size):
    copies = jnp.broadcast_to(piece[None], (size,) + piece.shape)
    return copies.reshape((size * piece.shape[0],) + piece.shape[1:])


def spread(piece):
    return lax.all_to_all(copies_of(piece, lax.axis_size("col")), "col", 0, 0, tiled=True)


def spread_half(piece):
    size = lax.axis_size("row")
    groups = [list(range(core, size, 2)) for core in range(2)]
    copies = copies_of(piece, size // 2)
    return lax.all_to_all(copies, "row", 0, 0, axis_index_groups=groups, tiled=True)


def swap(piece, row_of):
    size = lax.axis_size("row")
    pairs = [(a * size + b, row_of(b) * size + a) for a in range(size) for b in range(size)]
    return lax.ppermute(piece, ("row", "col"), pairs)


def partner(held, bit):
    size = lax.axis_size("row")
    return lax.ppermute(held, "row", [(r, r ^ bit) for r in range(size)])


def on_device(three_index, pair_list, block_offsets, block_count, coefficients):
    size = lax.axis_size("row")
    part = coefficients.shape[0] // size
    row = lax.axis_index("row").astype(jnp.int32).reshape(1)

    own_coef = lax.dynamic_slice_in_dim(coefficients, lax.axis_index("col") * part, part, 0)
    coef_half = spread_half(swap(own_coef, lambda b: 2 * (b % (size // 2)) + b // (size // 2)))
    term = tile_term(
        three_index,
        pair_list,
        block_offsets,
        block_count,
        row % 2,
        coef_half,
        partner(coef_half, 1),
    )

    received = lax.all_to_all(term, "col", 0, 0, tiled=True)
    received = received.reshape((size, part, term.shape[1]))
    factor = jnp.sum(received, axis=0, dtype=jnp.float32).astype(jnp.bfloat16)

    row_factor = spread(factor)
    held = swap(factor, lambda b: b)
    for bit in DOUBLING:
        held = jnp.concatenate([held, partner(held, bit)], axis=0)
    return exchange_tile(row, row_factor, held, partner(held, 1))


def solution(mesh):
    return jax.shard_map(
        on_device,
        mesh=mesh,
        in_specs=(
            P("row", "col", None, None, None, None),
            P("row", "col", None),
            P("row", "col", None),
            P("row", "col"),
            P("row", None),
        ),
        out_specs=P("row", "col"),
        check_vma=False,
    )
```

```python
import jax
import jax.numpy as jnp
from jax import lax
from jax.experimental import pallas as pl
from jax.experimental.pallas import tpu as pltpu
from jax.sharding import PartitionSpec as P

DOUBLING = (16, 8, 4, 2)
PIECES = 1 << len(DOUBLING)
VMEM_LIMIT = 20 * 1024 * 1024


def member_bits(place):
    return sum(bit for k, bit in enumerate(DOUBLING) if place >> k & 1)


def tile_term_kernel(
    pair_ref, offset_ref, count_ref, core_ref, blocks_ref, mine_ref, other_ref, term_ref, total
):
    _, _, slot_total, aux_count, width, _ = blocks_ref.shape
    half, orbitals = mine_ref.shape
    in_half = half // width
    total[...] = jnp.zeros_like(total)
    for slot in range(slot_total):

        @pl.when(slot < count_ref[0, 0])
        def _():
            block = pair_ref[0, 0, slot]
            first = pl.multiple_of(lax.rem(block, in_half) * width, width)
            offset = pl.multiple_of(offset_ref[0, 0, slot], width)
            nu_rows = jnp.where(
                lax.div(block, in_half) == core_ref[0],
                mine_ref[pl.ds(first, width), :],
                other_ref[pl.ds(first, width), :],
            )
            for p in range(aux_count):
                columns = slice(p * orbitals, (p + 1) * orbitals)
                total[pl.ds(offset, width), columns] += jnp.dot(
                    blocks_ref[0, 0, slot, p], nu_rows, preferred_element_type=jnp.float32
                )

    term_ref[...] = total[...].astype(term_ref.dtype)


def tile_term(blocks, pairs, offsets, count, core, mine, other):
    rows, columns = 2 * mine.shape[0], blocks.shape[3] * mine.shape[1]
    smem = pl.BlockSpec(memory_space=pltpu.SMEM)
    vmem = pl.BlockSpec(memory_space=pltpu.VMEM)
    return pl.pallas_call(
        tile_term_kernel,
        out_shape=jax.ShapeDtypeStruct((rows, columns), jnp.bfloat16),
        in_specs=[smem, smem, smem, smem, vmem, vmem, vmem],
        out_specs=vmem,
        scratch_shapes=[pltpu.VMEM((rows, columns), jnp.float32)],
        compiler_params=pltpu.CompilerParams(vmem_limit_bytes=VMEM_LIMIT),
    )(pairs, offsets, count, core, blocks, mine, other)


def exchange_kernel(row_ref, row_factor_ref, mine_ref, other_ref, out_ref, col_factor):
    piece = col_factor.shape[0] // (2 * PIECES)

    @pl.when(pl.program_id(0) == 0)
    def _():
        for place in range(PIECES):
            member = row_ref[0] ^ member_bits(place)
            for held_ref, at in ((mine_ref, member), (other_ref, member ^ 1)):
                rows = pl.ds(pl.multiple_of(at * piece, piece), piece)
                col_factor[rows, :] = held_ref[place * piece : (place + 1) * piece, :]

    out_ref[...] = lax.dot_general(
        row_factor_ref[...],
        col_factor[...],
        (((1,), (1,)), ((), ())),
        preferred_element_type=jnp.float32,
    ).astype(out_ref.dtype)


def exchange_tile(row, row_factor, mine, other):
    rows, depth = row_factor.shape
    columns = 2 * mine.shape[0]
    step = rows // 4
    vmem = pl.BlockSpec(memory_space=pltpu.VMEM)
    return pl.pallas_call(
        exchange_kernel,
        grid=(rows // step,),
        out_shape=jax.ShapeDtypeStruct((rows, columns), jnp.bfloat16),
        in_specs=[
            pl.BlockSpec(memory_space=pltpu.SMEM),
            pl.BlockSpec((step, depth), lambda i: (i, 0)),
            vmem,
            vmem,
        ],
        out_specs=pl.BlockSpec((step, columns), lambda i: (i, 0)),
        scratch_shapes=[pltpu.VMEM((columns, depth), jnp.bfloat16)],
        compiler_params=pltpu.CompilerParams(vmem_limit_bytes=VMEM_LIMIT),
    )(row, row_factor, mine, other)


def copies_of(piece, size):
    copies = jnp.broadcast_to(piece[None], (size,) + piece.shape)
    return copies.reshape((size * piece.shape[0],) + piece.shape[1:])


def spread(piece):
    return lax.all_to_all(copies_of(piece, lax.axis_size("col")), "col", 0, 0, tiled=True)


def spread_half(piece):
    size = lax.axis_size("row")
    groups = [list(range(core, size, 2)) for core in range(2)]
    copies = copies_of(piece, size // 2)
    return lax.all_to_all(copies, "row", 0, 0, axis_index_groups=groups, tiled=True)


def swap(piece, row_of):
    size = lax.axis_size("row")
    pairs = [(a * size + b, row_of(b) * size + a) for a in range(size) for b in range(size)]
    return lax.ppermute(piece, ("row", "col"), pairs)


def partner(held, bit):
    size = lax.axis_size("row")
    return lax.ppermute(held, "row", [(r, r ^ bit) for r in range(size)])


def on_device(three_index, pair_list, block_offsets, block_count, coefficients):
    size = lax.axis_size("row")
    part = coefficients.shape[0] // size
    row = lax.axis_index("row").astype(jnp.int32).reshape(1)

    own_coef = lax.dynamic_slice_in_dim(coefficients, lax.axis_index("col") * part, part, 0)
    coef_half = spread_half(swap(own_coef, lambda b: 2 * (b % (size // 2)) + b // (size // 2)))
    term = tile_term(
        three_index,
        pair_list,
        block_offsets,
        block_count,
        row % 2,
        coef_half,
        partner(coef_half, 1),
    )

    received = lax.all_to_all(term, "col", 0, 0, tiled=True)
    received = received.reshape((size, part, term.shape[1]))
    factor = jnp.sum(received, axis=0, dtype=jnp.float32).astype(jnp.bfloat16)

    held, factor = lax.optimization_barrier((swap(factor, lambda b: b), factor))
    row_factor = spread(factor)
    for bit in DOUBLING:
        held = jnp.concatenate([held, partner(held, bit)], axis=0)
    return exchange_tile(row, row_factor, held, partner(held, 1))


def solution(mesh):
    return jax.shard_map(
        on_device,
        mesh=mesh,
        in_specs=(
            P("row", "col", None, None, None, None),
            P("row", "col", None),
            P("row", "col", None),
            P("row", "col"),
            P("row", None),
        ),
        out_specs=P("row", "col"),
        check_vma=False,
    )
```

```python
import jax
import jax.numpy as jnp
from jax import lax
from jax.experimental import pallas as pl
from jax.experimental.pallas import tpu as pltpu
from jax.sharding import PartitionSpec as P

NEAR = 4
DOUBLING = (2, 16, 8, 4)
PIECES = 1 << len(DOUBLING)
NOTE_ROWS = 16
VMEM_LIMIT = 20 * 1024 * 1024


def member_bits(place):
    return sum(bit for k, bit in enumerate(DOUBLING) if place >> k & 1)


def term_kernel(row_ref, col_ref, note_ref, *refs):
    slab_refs, (mine_ref, other_ref, term_ref, total) = refs[:NEAR], refs[NEAR:]
    slot_total = note_ref.shape[1] // 2
    orbitals = mine_ref.shape[1]
    width = slab_refs[0].shape[1]
    aux_count = total.shape[1] // orbitals
    rows = width // NEAR
    total[...] = jnp.zeros_like(total)
    for k, slab_ref in enumerate(slab_refs):
        tile = lax.rem(col_ref[0] + NEAR - k, NEAR)
        for slot in range(slot_total):

            @pl.when(slot < note_ref[k, 2 * slot_total])
            def _():
                place = note_ref[k, slot] * (NEAR // 2) + lax.div(tile, 2)
                first = pl.multiple_of(place * width, width)
                nu_rows = jnp.where(
                    lax.rem(tile, 2) == lax.rem(row_ref[0], 2),
                    mine_ref[pl.ds(first, width), :],
                    other_ref[pl.ds(first, width), :],
                )
                part = jnp.dot(
                    slab_ref[slot * width : (slot + 1) * width, :],
                    nu_rows,
                    preferred_element_type=jnp.float32,
                )
                offset = pl.multiple_of(note_ref[k, slot_total + slot] * rows, rows)
                for p in range(aux_count):
                    columns = slice(p * orbitals, (p + 1) * orbitals)
                    total[pl.ds(offset, rows), columns] += part[p * rows : (p + 1) * rows, :]

    term_ref[...] = total[...].astype(term_ref.dtype)


def near_term(row, col, notes, slabs, mine, other, rows, aux_count):
    columns = aux_count * mine.shape[1]
    smem = pl.BlockSpec(memory_space=pltpu.SMEM)
    vmem = pl.BlockSpec(memory_space=pltpu.VMEM)
    return pl.pallas_call(
        term_kernel,
        out_shape=jax.ShapeDtypeStruct((rows, columns), jnp.bfloat16),
        in_specs=[smem] * 3 + [vmem] * (NEAR + 2),
        out_specs=vmem,
        scratch_shapes=[pltpu.VMEM((rows, columns), jnp.float32)],
        compiler_params=pltpu.CompilerParams(vmem_limit_bytes=VMEM_LIMIT),
    )(row, col, notes, *slabs, mine, other)


def exchange_kernel(row_ref, row_factor_ref, mine_ref, other_ref, out_ref, col_factor, sems):
    piece = col_factor.shape[0] // (2 * PIECES)

    @pl.when(pl.program_id(0) == 0)
    def _():
        copies = []
        for place in range(PIECES):
            member = row_ref[0] ^ member_bits(place)
            for k, (held_ref, at) in enumerate(((mine_ref, member), (other_ref, member ^ 1))):
                rows = pl.ds(pl.multiple_of(at * piece, piece), piece)
                source = held_ref.at[pl.ds(place * piece, piece), :]
                copies.append(
                    pltpu.make_async_copy(source, col_factor.at[rows, :], sems.at[k, place])
                )
        for copy in copies:
            copy.start()
        for copy in copies:
            copy.wait()

    out_ref[...] = lax.dot_general(
        row_factor_ref[...],
        col_factor[...],
        (((1,), (1,)), ((), ())),
        preferred_element_type=jnp.float32,
    ).astype(out_ref.dtype)


def exchange_tile(row, row_factor, mine, other):
    rows, depth = row_factor.shape
    columns = 2 * mine.shape[0]
    step = rows // 4
    anywhere = pl.BlockSpec(memory_space=pl.ANY)
    return pl.pallas_call(
        exchange_kernel,
        grid=(rows // step,),
        out_shape=jax.ShapeDtypeStruct((rows, columns), jnp.bfloat16),
        in_specs=[
            pl.BlockSpec(memory_space=pltpu.SMEM),
            pl.BlockSpec((step, depth), lambda i: (i, 0)),
            anywhere,
            anywhere,
        ],
        out_specs=pl.BlockSpec((step, columns), lambda i: (i, 0)),
        scratch_shapes=[
            pltpu.VMEM((columns, depth), jnp.bfloat16),
            pltpu.SemaphoreType.DMA((2, PIECES)),
        ],
        compiler_params=pltpu.CompilerParams(vmem_limit_bytes=VMEM_LIMIT),
    )(row, row_factor, mine, other)


def copies_of(piece, size):
    copies = jnp.broadcast_to(piece[None], (size,) + piece.shape)
    return copies.reshape((size * piece.shape[0],) + piece.shape[1:])


def swap(piece, target):
    size = lax.axis_size("row")
    pairs = []
    for a in range(size):
        for b in range(size):
            r, c = target(a, b)
            pairs.append((a * size + b, r * size + c))
    return lax.ppermute(piece, ("row", "col"), pairs)


def partner(held, bit):
    size = lax.axis_size("row")
    return lax.ppermute(held, "row", [(r, r ^ bit) for r in range(size)])


def near_slabs(blocks, notes, col, coef_piece):
    size = lax.axis_size("col")
    slots, aux_count, width, depth = blocks.shape
    rows = width // NEAR
    slabs = []
    for k in range(NEAR):
        slab = lax.dynamic_slice_in_dim(blocks, lax.rem(col + k, NEAR) * rows, rows, 2)
        slab = slab.reshape(slots * aux_count * rows, depth)
        slabs.append(jnp.concatenate([slab, notes], axis=0))
    coef_piece, slabs = lax.optimization_barrier((coef_piece, slabs))
    for k in range(1, NEAR):
        pairs = [(c, c - c % NEAR + (c + k) % NEAR) for c in range(size)]
        slabs[k] = lax.ppermute(slabs[k], "col", pairs)
    return coef_piece, slabs


def on_device(three_index, pair_list, block_offsets, block_count, coefficients):
    size = lax.axis_size("row")
    far = size // NEAR
    blocks = three_index[0, 0]
    slots, aux_count, width, depth = blocks.shape
    part = coefficients.shape[0] // size
    row, col = (lax.axis_index(axis).astype(jnp.int32) for axis in ("row", "col"))

    piece_rows = coefficients.shape[0] // far
    own_coef = lax.dynamic_slice_in_dim(coefficients, lax.div(col, NEAR) * piece_rows, piece_rows, 0)
    coef_piece = swap(
        own_coef,
        lambda a, b: (b // NEAR * NEAR + a % NEAR, a // NEAR * NEAR + b % NEAR),
    )
    notes = jnp.concatenate([pair_list[0, 0], block_offsets[0, 0] // width, block_count[0]])
    notes = jnp.pad(notes.astype(jnp.bfloat16)[None], ((0, NOTE_ROWS - 1), (0, depth - 2 * slots - 1)))
    coef_piece, slabs = near_slabs(blocks, notes, col, coef_piece)
    near_notes = jnp.stack([slab[-NOTE_ROWS, : 2 * slots + 1] for slab in slabs]).astype(jnp.int32)

    same_core = [list(range(core, size, 2)) for core in range(2)]
    coef_half = lax.all_to_all(
        copies_of(coef_piece, size // 2), "row", 0, 0, axis_index_groups=same_core, tiled=True
    )
    term = near_term(
        row.reshape(1),
        col.reshape(1),
        near_notes,
        slabs,
        coef_half,
        partner(coef_half, 1),
        coefficients.shape[0] // NEAR,
        aux_count,
    )

    same_near = [list(range(near, size, NEAR)) for near in range(NEAR)]
    received = lax.all_to_all(term, "col", 0, 0, axis_index_groups=same_near, tiled=True)
    received = received.reshape((far, part, term.shape[1]))
    factor = jnp.sum(received, axis=0, dtype=jnp.float32).astype(jnp.bfloat16)

    held = swap(factor, lambda a, b: (b, a))
    held = jnp.concatenate([held, partner(held, DOUBLING[0])], axis=0)
    held, factor = lax.optimization_barrier((held, factor))
    row_factor = lax.all_to_all(copies_of(factor, size), "col", 0, 0, tiled=True)
    for bit in DOUBLING[1:]:
        held = jnp.concatenate([held, partner(held, bit)], axis=0)
    return exchange_tile(row.reshape(1), row_factor, held, partner(held, 1))


def solution(mesh):
    return jax.shard_map(
        on_device,
        mesh=mesh,
        in_specs=(
            P("row", "col", None, None, None, None),
            P("row", "col", None),
            P("row", "col", None),
            P("row", "col"),
            P("row", None),
        ),
        out_specs=P("row", "col"),
        check_vma=False,
    )
```

```python
import jax
import jax.numpy as jnp
from jax import lax
from jax.experimental import pallas as pl
from jax.experimental.pallas import tpu as pltpu
from jax.sharding import PartitionSpec as P

NEAR = 4
DOUBLING = (2, 16, 8, 4)
PIECES = 1 << len(DOUBLING)
NOTE_ROWS = 16
VMEM_LIMIT = 20 * 1024 * 1024


def member_bits(place):
    return sum(bit for k, bit in enumerate(DOUBLING) if place >> k & 1)


def term_kernel(row_ref, col_ref, note_ref, *refs):
    slab_refs, (mine_ref, other_ref, term_ref, total) = refs[:NEAR], refs[NEAR:]
    slot_total = note_ref.shape[1] // 2
    orbitals = mine_ref.shape[1]
    width = slab_refs[0].shape[1]
    aux_count = total.shape[1] // orbitals
    rows = width // NEAR
    total[...] = jnp.zeros_like(total)
    for k, slab_ref in enumerate(slab_refs):
        tile = lax.rem(col_ref[0] + NEAR - k, NEAR)
        for slot in range(slot_total):

            @pl.when(slot < note_ref[k, 2 * slot_total])
            def _():
                place = note_ref[k, slot] * (NEAR // 2) + lax.div(tile, 2)
                first = pl.multiple_of(place * width, width)
                nu_rows = jnp.where(
                    lax.rem(tile, 2) == lax.rem(row_ref[0], 2),
                    mine_ref[pl.ds(first, width), :],
                    other_ref[pl.ds(first, width), :],
                )
                part = jnp.dot(
                    slab_ref[slot * width : (slot + 1) * width, :],
                    nu_rows,
                    preferred_element_type=jnp.float32,
                )
                offset = pl.multiple_of(note_ref[k, slot_total + slot] * rows, rows)
                for p in range(aux_count):
                    columns = slice(p * orbitals, (p + 1) * orbitals)
                    total[pl.ds(offset, rows), columns] += part[p * rows : (p + 1) * rows, :]

    term_ref[...] = total[...].astype(term_ref.dtype)


def near_term(row, col, notes, slabs, mine, other, rows, aux_count):
    columns = aux_count * mine.shape[1]
    smem = pl.BlockSpec(memory_space=pltpu.SMEM)
    vmem = pl.BlockSpec(memory_space=pltpu.VMEM)
    return pl.pallas_call(
        term_kernel,
        out_shape=jax.ShapeDtypeStruct((rows, columns), jnp.bfloat16),
        in_specs=[smem] * 3 + [vmem] * (NEAR + 2),
        out_specs=vmem,
        scratch_shapes=[pltpu.VMEM((rows, columns), jnp.float32)],
        compiler_params=pltpu.CompilerParams(vmem_limit_bytes=VMEM_LIMIT),
    )(row, col, notes, *slabs, mine, other)


def exchange_kernel(row_ref, row_factor_ref, mine_ref, other_ref, out_ref, col_factor):
    piece = col_factor.shape[0] // (2 * PIECES)

    @pl.when(pl.program_id(0) == 0)
    def _():
        for place in range(PIECES):
            member = row_ref[0] ^ member_bits(place)
            for held_ref, at in ((mine_ref, member), (other_ref, member ^ 1)):
                rows = pl.ds(pl.multiple_of(at * piece, piece), piece)
                col_factor[rows, :] = held_ref[place * piece : (place + 1) * piece, :]

    out_ref[...] = lax.dot_general(
        row_factor_ref[...],
        col_factor[...],
        (((1,), (1,)), ((), ())),
        preferred_element_type=jnp.float32,
    ).astype(out_ref.dtype)


def exchange_tile(row, row_factor, mine, other):
    rows, depth = row_factor.shape
    columns = 2 * mine.shape[0]
    step = rows // 4
    vmem = pl.BlockSpec(memory_space=pltpu.VMEM)
    return pl.pallas_call(
        exchange_kernel,
        grid=(rows // step,),
        out_shape=jax.ShapeDtypeStruct((rows, columns), jnp.bfloat16),
        in_specs=[
            pl.BlockSpec(memory_space=pltpu.SMEM),
            pl.BlockSpec((step, depth), lambda i: (i, 0)),
            vmem,
            vmem,
        ],
        out_specs=pl.BlockSpec((step, columns), lambda i: (i, 0)),
        scratch_shapes=[pltpu.VMEM((columns, depth), jnp.bfloat16)],
        compiler_params=pltpu.CompilerParams(vmem_limit_bytes=VMEM_LIMIT),
    )(row, row_factor, mine, other)


def copies_of(piece, size):
    copies = jnp.broadcast_to(piece[None], (size,) + piece.shape)
    return copies.reshape((size * piece.shape[0],) + piece.shape[1:])


def swap(piece, target):
    size = lax.axis_size("row")
    pairs = []
    for a in range(size):
        for b in range(size):
            r, c = target(a, b)
            pairs.append((a * size + b, r * size + c))
    return lax.ppermute(piece, ("row", "col"), pairs)


def partner(held, bit):
    size = lax.axis_size("row")
    return lax.ppermute(held, "row", [(r, r ^ bit) for r in range(size)])


def near_slabs(blocks, notes, col, coef_piece):
    size = lax.axis_size("col")
    slots, aux_count, width, depth = blocks.shape
    rows = width // NEAR
    slabs = []
    for k in range(NEAR):
        slab = lax.dynamic_slice_in_dim(blocks, lax.rem(col + k, NEAR) * rows, rows, 2)
        slab = slab.reshape(slots * aux_count * rows, depth)
        slabs.append(jnp.concatenate([slab, notes], axis=0))
    coef_piece, slabs = lax.optimization_barrier((coef_piece, slabs))
    for k in range(1, NEAR):
        pairs = [(c, c - c % NEAR + (c + k) % NEAR) for c in range(size)]
        slabs[k] = lax.ppermute(slabs[k], "col", pairs)
    return coef_piece, slabs


def on_device(three_index, pair_list, block_offsets, block_count, coefficients):
    size = lax.axis_size("row")
    far = size // NEAR
    blocks = three_index[0, 0]
    slots, aux_count, width, depth = blocks.shape
    part = coefficients.shape[0] // size
    row, col = (lax.axis_index(axis).astype(jnp.int32) for axis in ("row", "col"))

    piece_rows = coefficients.shape[0] // far
    own_coef = lax.dynamic_slice_in_dim(coefficients, lax.div(col, NEAR) * piece_rows, piece_rows, 0)
    coef_piece = swap(
        own_coef,
        lambda a, b: (b // NEAR * NEAR + a % NEAR, a // NEAR * NEAR + b % NEAR),
    )
    notes = jnp.concatenate([pair_list[0, 0], block_offsets[0, 0] // width, block_count[0]])
    notes = jnp.pad(notes.astype(jnp.bfloat16)[None], ((0, NOTE_ROWS - 1), (0, depth - 2 * slots - 1)))
    coef_piece, slabs = near_slabs(blocks, notes, col, coef_piece)

    same_core = [list(range(core, size, 2)) for core in range(2)]
    coef_half = lax.all_to_all(
        copies_of(coef_piece, size // 2), "row", 0, 0, axis_index_groups=same_core, tiled=True
    )
    coef_half, slabs = lax.optimization_barrier((coef_half, slabs))
    near_notes = jnp.stack([slab[-NOTE_ROWS, : 2 * slots + 1] for slab in slabs]).astype(jnp.int32)
    term = near_term(
        row.reshape(1),
        col.reshape(1),
        near_notes,
        slabs,
        coef_half,
        partner(coef_half, 1),
        coefficients.shape[0] // NEAR,
        aux_count,
    )

    same_near = [list(range(near, size, NEAR)) for near in range(NEAR)]
    received = lax.all_to_all(term, "col", 0, 0, axis_index_groups=same_near, tiled=True)
    received = received.reshape((far, part, term.shape[1]))
    factor = jnp.sum(received, axis=0, dtype=jnp.float32).astype(jnp.bfloat16)

    held = swap(factor, lambda a, b: (b, a))
    held = jnp.concatenate([held, partner(held, DOUBLING[0])], axis=0)
    held, factor = lax.optimization_barrier((held, factor))
    row_factor = lax.all_to_all(copies_of(factor, size), "col", 0, 0, tiled=True)
    for bit in DOUBLING[1:]:
        held = jnp.concatenate([held, partner(held, bit)], axis=0)
    return exchange_tile(row.reshape(1), row_factor, held, partner(held, 1))


def solution(mesh):
    return jax.shard_map(
        on_device,
        mesh=mesh,
        in_specs=(
            P("row", "col", None, None, None, None),
            P("row", "col", None),
            P("row", "col", None),
            P("row", "col"),
            P("row", None),
        ),
        out_specs=P("row", "col"),
        check_vma=False,
    )
```

```python
import jax
import jax.numpy as jnp
from jax import lax
from jax.experimental import pallas as pl
from jax.experimental.pallas import tpu as pltpu
from jax.sharding import PartitionSpec as P

NEAR = 4
DOUBLING = (2, 16, 8, 4)
PIECES = 1 << len(DOUBLING)
NOTE_ROWS = 16
VMEM_LIMIT = 20 * 1024 * 1024


def member_bits(place):
    return sum(bit for k, bit in enumerate(DOUBLING) if place >> k & 1)


def term_kernel(row_ref, col_ref, note_ref, *refs):
    slab_refs, (mine_ref, other_ref, term_ref, total) = refs[:NEAR], refs[NEAR:]
    slot_total = note_ref.shape[1] // 2
    orbitals = mine_ref.shape[1]
    width = slab_refs[0].shape[1]
    aux_count = total.shape[1] // orbitals
    rows = width // NEAR
    total[...] = jnp.zeros_like(total)
    for k, slab_ref in enumerate(slab_refs):
        tile = lax.rem(col_ref[0] + NEAR - k, NEAR)
        for slot in range(slot_total):

            @pl.when(slot < note_ref[k, 2 * slot_total])
            def _():
                place = note_ref[k, slot] * (NEAR // 2) + lax.div(tile, 2)
                first = pl.multiple_of(place * width, width)
                nu_rows = jnp.where(
                    lax.rem(tile, 2) == lax.rem(row_ref[0], 2),
                    mine_ref[pl.ds(first, width), :],
                    other_ref[pl.ds(first, width), :],
                )
                part = jnp.dot(
                    slab_ref[slot * width : (slot + 1) * width, :],
                    nu_rows,
                    preferred_element_type=jnp.float32,
                )
                offset = pl.multiple_of(note_ref[k, slot_total + slot] * rows, rows)
                for p in range(aux_count):
                    columns = slice(p * orbitals, (p + 1) * orbitals)
                    total[pl.ds(offset, rows), columns] += part[p * rows : (p + 1) * rows, :]

    term_ref[...] = total[...].astype(term_ref.dtype)


def near_term(row, col, notes, slabs, mine, other, rows, aux_count):
    columns = aux_count * mine.shape[1]
    smem = pl.BlockSpec(memory_space=pltpu.SMEM)
    vmem = pl.BlockSpec(memory_space=pltpu.VMEM)
    return pl.pallas_call(
        term_kernel,
        out_shape=jax.ShapeDtypeStruct((rows, columns), jnp.bfloat16),
        in_specs=[smem] * 3 + [vmem] * (NEAR + 2),
        out_specs=vmem,
        scratch_shapes=[pltpu.VMEM((rows, columns), jnp.float32)],
        compiler_params=pltpu.CompilerParams(vmem_limit_bytes=VMEM_LIMIT),
    )(row, col, notes, *slabs, mine, other)


def exchange_kernel(row_ref, col_ref, row_factor_ref, mine_ref, other_ref, out_ref, col_factor):
    piece = col_factor.shape[0] // (2 * PIECES)

    @pl.when(pl.program_id(0) == 0)
    def _():
        for place in range(PIECES):
            member = row_ref[0] ^ member_bits(place)
            for held_ref, at in ((mine_ref, member), (other_ref, member ^ 1)):
                rows = pl.ds(pl.multiple_of(at * piece, piece), piece)
                col_factor[rows, :] = held_ref[place * piece : (place + 1) * piece, :]

    product = lax.dot_general(
        row_factor_ref[...],
        col_factor[...],
        (((1,), (1,)), ((), ())),
        preferred_element_type=jnp.float32,
    ).astype(out_ref.dtype)
    near = lax.rem(col_ref[0], NEAR)
    for place in range(product.shape[0] // piece):
        at = place // NEAR * NEAR + (near ^ place % NEAR)
        rows = pl.ds(pl.multiple_of(at * piece, piece), piece)
        out_ref[rows, :] = product[place * piece : (place + 1) * piece, :]


def exchange_tile(row, col, row_factor, mine, other):
    rows, depth = row_factor.shape
    columns = 2 * mine.shape[0]
    step = rows // 4
    vmem = pl.BlockSpec(memory_space=pltpu.VMEM)
    return pl.pallas_call(
        exchange_kernel,
        grid=(rows // step,),
        out_shape=jax.ShapeDtypeStruct((rows, columns), jnp.bfloat16),
        in_specs=[
            pl.BlockSpec(memory_space=pltpu.SMEM),
            pl.BlockSpec(memory_space=pltpu.SMEM),
            pl.BlockSpec((step, depth), lambda i: (i, 0)),
            vmem,
            vmem,
        ],
        out_specs=pl.BlockSpec((step, columns), lambda i: (i, 0)),
        scratch_shapes=[pltpu.VMEM((columns, depth), jnp.bfloat16)],
        compiler_params=pltpu.CompilerParams(vmem_limit_bytes=VMEM_LIMIT),
    )(row, col, row_factor, mine, other)


def copies_of(piece, size):
    copies = jnp.broadcast_to(piece[None], (size,) + piece.shape)
    return copies.reshape((size * piece.shape[0],) + piece.shape[1:])


def swap(piece, target):
    size = lax.axis_size("row")
    pairs = []
    for a in range(size):
        for b in range(size):
            r, c = target(a, b)
            pairs.append((a * size + b, r * size + c))
    return lax.ppermute(piece, ("row", "col"), pairs)


def partner(held, bit):
    size = lax.axis_size("row")
    return lax.ppermute(held, "row", [(r, r ^ bit) for r in range(size)])


def near_partner(piece, bits):
    size = lax.axis_size("col")
    return lax.ppermute(piece, "col", [(c, c ^ bits) for c in range(size)])


def near_slabs(blocks, notes, col, coef_piece):
    size = lax.axis_size("col")
    slots, aux_count, width, depth = blocks.shape
    rows = width // NEAR
    slabs = []
    for k in range(NEAR):
        slab = lax.dynamic_slice_in_dim(blocks, lax.rem(col + k, NEAR) * rows, rows, 2)
        slab = slab.reshape(slots * aux_count * rows, depth)
        slabs.append(jnp.concatenate([slab, notes], axis=0))
    coef_piece, slabs = lax.optimization_barrier((coef_piece, slabs))
    for k in range(1, NEAR):
        pairs = [(c, c - c % NEAR + (c + k) % NEAR) for c in range(size)]
        slabs[k] = lax.ppermute(slabs[k], "col", pairs)
    return coef_piece, slabs


def on_device(three_index, pair_list, block_offsets, block_count, coefficients):
    size = lax.axis_size("row")
    far = size // NEAR
    blocks = three_index[0, 0]
    slots, aux_count, width, depth = blocks.shape
    part = coefficients.shape[0] // size
    row, col = (lax.axis_index(axis).astype(jnp.int32) for axis in ("row", "col"))

    piece_rows = coefficients.shape[0] // far
    own_coef = lax.dynamic_slice_in_dim(coefficients, lax.div(col, NEAR) * piece_rows, piece_rows, 0)
    coef_piece = swap(
        own_coef,
        lambda a, b: (b // NEAR * NEAR + a % NEAR, a // NEAR * NEAR + b % NEAR),
    )
    notes = jnp.concatenate([pair_list[0, 0], block_offsets[0, 0] // width, block_count[0]])
    notes = jnp.pad(notes.astype(jnp.bfloat16)[None], ((0, NOTE_ROWS - 1), (0, depth - 2 * slots - 1)))
    coef_piece, slabs = near_slabs(blocks, notes, col, coef_piece)

    same_core = [list(range(core, size, 2)) for core in range(2)]
    coef_half = lax.all_to_all(
        copies_of(coef_piece, size // 2), "row", 0, 0, axis_index_groups=same_core, tiled=True
    )
    coef_half, slabs = lax.optimization_barrier((coef_half, slabs))
    near_notes = jnp.stack([slab[-NOTE_ROWS, : 2 * slots + 1] for slab in slabs]).astype(jnp.int32)
    term = near_term(
        row.reshape(1),
        col.reshape(1),
        near_notes,
        slabs,
        coef_half,
        partner(coef_half, 1),
        coefficients.shape[0] // NEAR,
        aux_count,
    )

    same_near = [list(range(near, size, NEAR)) for near in range(NEAR)]
    received = lax.all_to_all(term, "col", 0, 0, axis_index_groups=same_near, tiled=True)
    received = received.reshape((far, part, term.shape[1]))
    factor = jnp.sum(received, axis=0, dtype=jnp.float32).astype(jnp.bfloat16)

    held = swap(factor, lambda a, b: (b, a))
    near = jnp.concatenate([factor] + [near_partner(factor, bits) for bits in range(1, NEAR)], axis=0)
    held, copies = lax.optimization_barrier((held, copies_of(near, far)))
    row_factor = lax.all_to_all(copies, "col", 0, 0, axis_index_groups=same_near, tiled=True)
    for bit in DOUBLING:
        held = jnp.concatenate([held, partner(held, bit)], axis=0)
    return exchange_tile(row.reshape(1), col.reshape(1), row_factor, held, partner(held, 1))


def solution(mesh):
    return jax.shard_map(
        on_device,
        mesh=mesh,
        in_specs=(
            P("row", "col", None, None, None, None),
            P("row", "col", None),
            P("row", "col", None),
            P("row", "col"),
            P("row", None),
        ),
        out_specs=P("row", "col"),
        check_vma=False,
    )
```

```python
import jax
import jax.numpy as jnp
from jax import lax
from jax.experimental import pallas as pl
from jax.experimental.pallas import tpu as pltpu
from jax.sharding import PartitionSpec as P

NEAR = 4
DOUBLING = (2, 16, 8, 4)
PIECES = 1 << len(DOUBLING)
NOTE_ROWS = 16
VMEM_LIMIT = 20 * 1024 * 1024


def member_bits(place):
    return sum(bit for k, bit in enumerate(DOUBLING) if place >> k & 1)


def term_kernel(row_ref, col_ref, note_ref, *refs):
    slab_refs, (mine_ref, other_ref, term_ref, total) = refs[:NEAR], refs[NEAR:]
    slot_total = note_ref.shape[1] // 2
    orbitals = mine_ref.shape[1]
    width = slab_refs[0].shape[1]
    aux_count = total.shape[1] // orbitals
    rows = width // NEAR
    total[...] = jnp.zeros_like(total)
    for k, slab_ref in enumerate(slab_refs):
        tile = lax.rem(col_ref[0] + NEAR - k, NEAR)
        for slot in range(slot_total):

            @pl.when(slot < note_ref[k, 2 * slot_total])
            def _():
                place = note_ref[k, slot] * (NEAR // 2) + lax.div(tile, 2)
                first = pl.multiple_of(place * width, width)
                nu_rows = jnp.where(
                    lax.rem(tile, 2) == lax.rem(row_ref[0], 2),
                    mine_ref[pl.ds(first, width), :],
                    other_ref[pl.ds(first, width), :],
                )
                part = jnp.dot(
                    slab_ref[slot * width : (slot + 1) * width, :],
                    nu_rows,
                    preferred_element_type=jnp.float32,
                )
                offset = pl.multiple_of(note_ref[k, slot_total + slot] * rows, rows)
                for p in range(aux_count):
                    columns = slice(p * orbitals, (p + 1) * orbitals)
                    total[pl.ds(offset, rows), columns] += part[p * rows : (p + 1) * rows, :]

    term_ref[...] = total[...].astype(term_ref.dtype)


def near_term(row, col, notes, slabs, mine, other, rows, aux_count):
    columns = aux_count * mine.shape[1]
    smem = pl.BlockSpec(memory_space=pltpu.SMEM)
    vmem = pl.BlockSpec(memory_space=pltpu.VMEM)
    return pl.pallas_call(
        term_kernel,
        out_shape=jax.ShapeDtypeStruct((rows, columns), jnp.bfloat16),
        in_specs=[smem] * 3 + [vmem] * (NEAR + 2),
        out_specs=vmem,
        scratch_shapes=[pltpu.VMEM((rows, columns), jnp.float32)],
        compiler_params=pltpu.CompilerParams(vmem_limit_bytes=VMEM_LIMIT),
    )(row, col, notes, *slabs, mine, other)


def exchange_kernel(row_ref, col_ref, row_factor_ref, mine_ref, other_ref, out_ref, col_factor):
    piece = col_factor.shape[0] // (2 * PIECES)

    @pl.when(pl.program_id(0) == 0)
    def _():
        for place in range(PIECES):
            member = row_ref[0] ^ member_bits(place)
            for held_ref, at in ((mine_ref, member), (other_ref, member ^ 1)):
                rows = pl.ds(pl.multiple_of(at * piece, piece), piece)
                col_factor[rows, :] = held_ref[place * piece : (place + 1) * piece, :]

    product = lax.dot_general(
        row_factor_ref[...],
        col_factor[...],
        (((1,), (1,)), ((), ())),
        preferred_element_type=jnp.float32,
    ).astype(out_ref.dtype)
    near = lax.rem(col_ref[0], NEAR)
    for place in range(product.shape[0] // piece):
        at = place // NEAR * NEAR + (near ^ place % NEAR)
        rows = pl.ds(pl.multiple_of(at * piece, piece), piece)
        out_ref[rows, :] = product[place * piece : (place + 1) * piece, :]


def exchange_tile(row, col, row_factor, mine, other):
    rows, depth = row_factor.shape
    columns = 2 * mine.shape[0]
    step = rows // 4
    vmem = pl.BlockSpec(memory_space=pltpu.VMEM)
    return pl.pallas_call(
        exchange_kernel,
        grid=(rows // step,),
        out_shape=jax.ShapeDtypeStruct((rows, columns), jnp.bfloat16),
        in_specs=[
            pl.BlockSpec(memory_space=pltpu.SMEM),
            pl.BlockSpec(memory_space=pltpu.SMEM),
            pl.BlockSpec((step, depth), lambda i: (i, 0)),
            vmem,
            vmem,
        ],
        out_specs=pl.BlockSpec((step, columns), lambda i: (i, 0)),
        scratch_shapes=[pltpu.VMEM((columns, depth), jnp.bfloat16)],
        compiler_params=pltpu.CompilerParams(vmem_limit_bytes=VMEM_LIMIT),
    )(row, col, row_factor, mine, other)


def copies_of(piece, size):
    copies = jnp.broadcast_to(piece[None], (size,) + piece.shape)
    return copies.reshape((size * piece.shape[0],) + piece.shape[1:])


def swap(piece, target):
    size = lax.axis_size("row")
    pairs = []
    for a in range(size):
        for b in range(size):
            r, c = target(a, b)
            pairs.append((a * size + b, r * size + c))
    return lax.ppermute(piece, ("row", "col"), pairs)


def partner(held, bit):
    size = lax.axis_size("row")
    return lax.ppermute(held, "row", [(r, r ^ bit) for r in range(size)])


def near_partner(piece, bits):
    size = lax.axis_size("col")
    return lax.ppermute(piece, "col", [(c, c ^ bits) for c in range(size)])


def near_slabs(blocks, notes, col, coef_piece):
    size = lax.axis_size("col")
    slots, aux_count, width, depth = blocks.shape
    rows = width // NEAR
    slabs = []
    for k in range(NEAR):
        slab = lax.dynamic_slice_in_dim(blocks, lax.rem(col + k, NEAR) * rows, rows, 2)
        slab = slab.reshape(slots * aux_count * rows, depth)
        slabs.append(jnp.concatenate([slab, notes], axis=0))
    coef_piece, slabs = lax.optimization_barrier((coef_piece, slabs))
    for k in range(1, NEAR):
        pairs = [(c, c - c % NEAR + (c + k) % NEAR) for c in range(size)]
        slabs[k] = lax.ppermute(slabs[k], "col", pairs)
    return coef_piece, slabs


def on_device(three_index, pair_list, block_offsets, block_count, coefficients):
    size = lax.axis_size("row")
    far = size // NEAR
    blocks = three_index[0, 0]
    slots, aux_count, width, depth = blocks.shape
    part = coefficients.shape[0] // size
    row, col = (lax.axis_index(axis).astype(jnp.int32) for axis in ("row", "col"))

    piece_rows = coefficients.shape[0] // far
    own_coef = lax.dynamic_slice_in_dim(coefficients, lax.div(col, NEAR) * piece_rows, piece_rows, 0)
    coef_piece = swap(
        own_coef,
        lambda a, b: (b // NEAR * NEAR + a % NEAR, a // NEAR * NEAR + b % NEAR),
    )
    notes = jnp.concatenate([pair_list[0, 0], block_offsets[0, 0] // width, block_count[0]])
    notes = jnp.pad(notes.astype(jnp.bfloat16)[None], ((0, NOTE_ROWS - 1), (0, depth - 2 * slots - 1)))
    coef_piece, slabs = near_slabs(blocks, notes, col, coef_piece)

    same_core = [list(range(core, size, 2)) for core in range(2)]
    coef_half = lax.all_to_all(
        copies_of(coef_piece, size // 2), "row", 0, 0, axis_index_groups=same_core, tiled=True
    )
    coef_half, slabs = lax.optimization_barrier((coef_half, slabs))
    near_notes = jnp.stack([slab[-NOTE_ROWS, : 2 * slots + 1] for slab in slabs]).astype(jnp.int32)
    term = near_term(
        row.reshape(1),
        col.reshape(1),
        near_notes,
        slabs,
        coef_half,
        partner(coef_half, 1),
        coefficients.shape[0] // NEAR,
        aux_count,
    )

    same_near = [list(range(near, size, NEAR)) for near in range(NEAR)]
    received = lax.all_to_all(term, "col", 0, 0, axis_index_groups=same_near, tiled=True)
    received = received.reshape((far, part, term.shape[1]))
    factor = jnp.sum(received, axis=0, dtype=jnp.float32).astype(jnp.bfloat16)

    held = swap(factor, lambda a, b: (b, a))
    near = jnp.concatenate([factor] + [near_partner(factor, bits) for bits in range(1, NEAR)], axis=0)
    held = jnp.concatenate([held, partner(held, DOUBLING[0])], axis=0)
    held, copies = lax.optimization_barrier((held, copies_of(near, far)))
    row_factor = lax.all_to_all(copies, "col", 0, 0, axis_index_groups=same_near, tiled=True)
    for bit in DOUBLING[1:]:
        held = jnp.concatenate([held, partner(held, bit)], axis=0)
    return exchange_tile(row.reshape(1), col.reshape(1), row_factor, held, partner(held, 1))


def solution(mesh):
    return jax.shard_map(
        on_device,
        mesh=mesh,
        in_specs=(
            P("row", "col", None, None, None, None),
            P("row", "col", None),
            P("row", "col", None),
            P("row", "col"),
            P("row", None),
        ),
        out_specs=P("row", "col"),
        check_vma=False,
    )
```
